256 devices in a mesh: dp: 8 (over x, core), pipe: 8 (over z), tensor: 4 (over y).
Axes of the slice: x: 4, y: 4, z: 8, core: 2. Of those that a mesh axis runs over, the one named last changes fastest.
Arguments:
- tokens: bfloat16 [4096, 4096], P(('dp', 'tensor')), parts along dimension 0, may hold values from -15 to 15
- grad_out: bfloat16 [4096, 4096], P(('dp', 'tensor')), parts along dimension 0, may hold values from -6 to 6
- w_in: bfloat16 [4096, 16384], P(None, ('pipe', 'tensor')), may hold values from -5 to 5
- w_out: bfloat16 [16384, 4096], P(('pipe', 'tensor')), may hold values from -1 to 1
Outputs:
- block_out: bfloat16 [4096, 4096], P(('dp', 'tensor')), parts along dimension 0
- grad_in: bfloat16 [4096, 4096], P(('dp', 'tensor')), parts along dimension 0
- log_peaks: float32 [32], P('dp'), parts along dimension 0
The draws below stay inside these ranges and needn't reach their ends.
There are 8 independent parts, one for each index of `dp`. The reference program is written for one: setup_inputs(seed, part) draws one part's arguments, and reference() takes and returns one part's arrays. A program takes and returns all parts, laid end to end along the dimension named above; an argument that names none is the same for every part. Nothing has to cross between parts.
All inputs are finite; a program needn't handle non-finite values.
Results may differ from the reference program's by a relative error of at most 0.0039.
Values may be sent and summed in bfloat16 or wider, within the bound.
A program may use at most 128 MiB of HBM per device.

```python
import math
import jax
import jax.numpy as jnp
from jax import lax

D = 4096
FF = 16384
TOKENS = 512


def draw_tokens(key, part):
    key = jax.random.fold_in(key, 5)
    base_key, row_key = jax.random.split(key)
    base = jax.random.truncated_normal(base_key, -6.0, 6.0, (TOKENS, D), jnp.float32)
    row_scale = jnp.exp(jax.random.uniform(row_key, (TOKENS,), jnp.float32, math.log(0.4), math.log(2.5)))
    return (base * row_scale[:, None]).astype(jnp.bfloat16)


def draw_w_in(key, part):
    key = jax.random.fold_in(key, 11)
    base_key, column_key = jax.random.split(key)
    base = jax.random.truncated_normal(base_key, -6.0, 6.0, (D, FF), jnp.float32)
    spread = jnp.exp(jax.random.uniform(column_key, (FF,), jnp.float32, math.log(0.5), math.log(2.0)))
    rising = jnp.exp(math.log(3.0) * jnp.arange(FF, dtype=jnp.float32) / FF)
    return (base * (spread * rising)[None, :] / math.sqrt(D)).astype(jnp.bfloat16)


def draw_w_out(key, part):
    key = jax.random.fold_in(key, 17)
    base_key, row_key = jax.random.split(key)
    base = jax.random.truncated_normal(base_key, -6.0, 6.0, (FF, D), jnp.float32)
    spread = jnp.exp(jax.random.uniform(row_key, (FF,), jnp.float32, math.log(0.6), math.log(1.6)))
    return (base * spread[:, None] * (0.048 / math.sqrt(FF))).astype(jnp.bfloat16)


def level_of(rng, dims, cuts, smallest, top_value):
    def one(dim, shards_of):
        draws = jax.random.uniform(jax.random.fold_in(jax.random.fold_in(rng, 6), dim), (shards_of,), jnp.float32, smallest / len(cuts), top_value / len(cuts))
        return jnp.repeat(jnp.exp(draws), dims[dim] // shards_of).reshape((-1,) + (1,) * (len(dims) - dim - 1))

    gain = one(*cuts[0])
    for cut in cuts[1:]:
        gain = gain * one(*cut)
    return gain


def noise(stream_key, shape, scale, reach, shards=(), kind=jnp.bfloat16):
    array = scale * jax.random.normal(stream_key, shape, jnp.float32)
    if shards:
        array = array * level_of(stream_key, shape, shards, -0.22, 0.18)
    return jnp.clip(array, -reach, reach).astype(kind)


def setup_inputs(seed: int = 0, part: int = 0) -> dict:
    seeds = jax.random.split(jax.random.key(seed), 5)
    part_keys = jax.random.split(jax.random.fold_in(seeds[4], part), 5)
    return {
        "tokens": draw_tokens(jax.random.fold_in(jax.random.fold_in(seeds[4], part), 71), part),
        "grad_out": noise(part_keys[1], (TOKENS, D), 1.0, 6.0, ((0, 4),)),
        "w_in": draw_w_in(jax.random.fold_in(seeds[4], 71), part),
        "w_out": draw_w_out(jax.random.fold_in(seeds[4], 71), part),
    }


def current_scale(peak_value, ceiling):
    return ceiling / (peak_value + 1e-6)


def grid_round(values, mantissa, lowest, ceiling):
    magnitude = jnp.abs(values)
    least_normal = 2.0 ** lowest
    exponent = jnp.floor(jnp.log2(jnp.maximum(magnitude, least_normal)))
    spacing = jnp.exp2(exponent - mantissa)
    snapped = jnp.minimum(jnp.floor(magnitude / spacing + 0.5) * spacing, ceiling)
    return jnp.where(values < 0.0, -snapped, snapped)


def reference(tokens, grad_out, w_in, w_out):
    pre_act = jnp.dot(tokens, w_in, preferred_element_type=jnp.float32)
    positive = jnp.maximum(pre_act, 0.0)
    hidden = positive * positive
    peak_hidden = jnp.max(hidden)
    scale_hidden = current_scale(peak_hidden, 448.0)
    hidden_q = grid_round(hidden * scale_hidden, 3, -6, 448.0).astype(jnp.bfloat16)
    block_out = (jnp.dot(hidden_q, w_out, preferred_element_type=jnp.float32) / scale_hidden).astype(jnp.bfloat16)
    hidden_grad = lax.dot_general(grad_out, w_out, (((1,), (1,)), ((), ())), preferred_element_type=jnp.float32)
    pre_grad = hidden_grad * 2.0 * positive
    peak_grad = jnp.max(jnp.abs(pre_grad))
    scale_grad = current_scale(peak_grad, 57344.0)
    grad_q = grid_round(pre_grad * scale_grad, 2, -14, 57344.0).astype(jnp.bfloat16)
    grad_in = lax.dot_general(grad_q, w_in, (((1,), (1,)), ((), ())), preferred_element_type=jnp.float32)
    grad_in = (grad_in / scale_grad).astype(jnp.bfloat16)
    token_peak = jnp.max(jnp.abs(tokens.astype(jnp.float32)))
    output_peak = jnp.max(jnp.abs(grad_out.astype(jnp.float32)))
    log_peaks = jnp.log(jnp.stack([token_peak, peak_hidden, output_peak, peak_grad]) + 1e-6)
    return block_out, grad_in, log_peaks
```

```python
import jax
import jax.numpy as jnp
from jax import lax
from jax.experimental import pallas as pl
from jax.experimental.pallas import tpu as pltpu
from jax.sharding import PartitionSpec as P

MESH = pl.DeviceIdType.MESH
F32, BF16 = jnp.float32, jnp.bfloat16
CHUNKS = 4
SLICES = 8
DMAS = 288


def snap(values, mantissa, lowest, ceiling):
    magnitude = jnp.abs(values)
    scaled = jnp.maximum(magnitude, 2.0**lowest) * (2.0**23 + 1.0)
    first = scaled - scaled * (1.0 - 2.0**-24)
    spacing = first * (2.0**-mantissa)
    magic = first * (1.5 * 2.0 ** (23 - mantissa))
    near = (magnitude + magic) - magic
    near = jnp.where(magnitude - near >= 0.5 * spacing, near + spacing, near)
    near = jnp.minimum(near, ceiling)
    return jnp.where(values < 0.0, -near, near)


def dot_nt(a, b):
    return lax.dot_general(a, b, (((1,), (1,)), ((), ())), preferred_element_type=F32)


def dot_nn(a, b):
    return jnp.dot(a, b, preferred_element_type=F32)


def kernel(
    tok_in, grd_in, wi_in, wo_in, out0, out1, peaks_out,
    tok, grd, wi0, wi1, wo0, wo1, pa, hg, hq, gq, acc0, acc1, ysend, yrecv,
    send_r, send_l, recv_r, recv_l, obuf, pk_send, pk_y, pk_z, local_sem, send_sem, recv_sem,
):
    dp, z, y = lax.axis_index("dp"), lax.axis_index("pipe"), lax.axis_index("tensor")
    core = lax.rem(dp, 2)
    rows, width = tok_in.shape
    ff = wi_in.shape[1]
    half = rows // 2
    sub = rows // 8
    cw = width // CHUNKS
    outs = (out0, out1)
    accs = (acc0, acc1)

    y_far = (dp, z, lax.rem(y + 2, 4))
    y_a = (dp, z, y + 1 - 2 * lax.rem(y, 2))
    y_b = (dp, z, 3 - y)
    x_right = (lax.rem(dp + 2, 8), z, y)
    x_left = (lax.rem(dp + 6, 8), z, y)
    other = (dp + 1 - 2 * core, z, y)
    z_at = [(dp, lax.rem(z + d, 8), y) for d in range(8)]
    y_at = [(dp, z, lax.rem(y + d, 4)) for d in range(4)]
    z_right, z_left = z_at[1], z_at[7]

    handles = {}
    unsent = []
    state = {"n": 0}
    events = []

    def at(t, fn, *args):
        events.append((t, len(events), fn, args))

    def send(name, src, dst, device):
        i = state["n"]
        state["n"] += 1
        copy = pltpu.make_async_remote_copy(
            src_ref=src, dst_ref=dst, send_sem=send_sem.at[i], recv_sem=recv_sem.at[i],
            device_id=device, device_id_type=MESH,
        )
        copy.start()
        handles[name] = i
        unsent.append(copy)

    def arrive(name, dst):
        i = handles[name]
        pltpu.make_async_remote_copy(
            src_ref=dst, dst_ref=dst, send_sem=send_sem.at[i], recv_sem=recv_sem.at[i],
            device_id=other, device_id_type=MESH,
        ).wait_recv()

    def drain(keep):
        while len(unsent) > keep:
            unsent.pop(0).wait_send()

    loads = [
        pltpu.make_async_copy(tok_in, tok.at[pl.ds(0, rows)], local_sem.at[0]),
        pltpu.make_async_copy(wi_in, wi0, local_sem.at[1]),
        pltpu.make_async_copy(grd_in, grd.at[pl.ds(0, rows)], local_sem.at[2]),
        pltpu.make_async_copy(wo_in, wo0, local_sem.at[3]),
    ]
    for load in loads:
        load.start()

    barrier = pltpu.get_barrier_semaphore()
    peers = [x_right, x_left, other] + y_at[1:] + z_at[1:]
    for peer in peers:
        pl.semaphore_signal(barrier, inc=1, device_id=peer, device_id_type=MESH)
    pl.semaphore_wait(barrier, len(peers))

    def region(k, s, part=None):
        if k < CHUNKS:
            n = cw // SLICES
            r0, c0, nc = k * cw + s * n, 0, ff
        else:
            n = ff // SLICES
            r0, c0, nc = s * n, (k - CHUNKS) * cw, cw
        if part is not None:
            n = n // 2
            r0 = r0 + part * n
        return pl.ds(pl.multiple_of(r0, 16), n), pl.ds(c0, nc)

    def slice_at(d, c):
        return 2 * lax.rem(lax.div(dp, 2) + d, 4) + c

    mine = slice_at(0, core)
    left, right, far = slice_at(3, core), slice_at(1, core), slice_at(2, core)

    def w_y(k):
        src, dst = (wi_in, wi1) if k < CHUNKS else (wo_in, wo1)
        at_ = region(k, mine)
        send(("wy", k), src.at[at_], dst.at[at_], y_far)

    def weight(k):
        return wi1 if k < CHUNKS else wo1

    def w_a(k):
        w, r = weight(k), region(k, mine)
        arrive(("wy", k), w.at[r])
        send(("xr", k), w.at[r], w.at[r], x_right)
        send(("xl", k), w.at[r], w.at[r], x_left)
        send(("c0", k), w.at[r], w.at[r], other)
        if k + 2 < 2 * CHUNKS:
            w_y(k + 2)

    def w_b(k):
        w = weight(k)
        r = region(k, left)
        arrive(("xr", k), w.at[r])
        p = region(k, left, 0)
        send(("dr", k), w.at[p], w.at[p], x_right)
        send(("c1", k), w.at[r], w.at[r], other)
        r = region(k, right)
        arrive(("xl", k), w.at[r])
        p = region(k, right, 1)
        send(("dl", k), w.at[p], w.at[p], x_left)
        send(("c2", k), w.at[r], w.at[r], other)

    def w_c(k):
        w = weight(k)
        arrive(("dr", k), w.at[region(k, far, 0)])
        arrive(("dl", k), w.at[region(k, far, 1)])
        r = region(k, far)
        send(("c3", k), w.at[r], w.at[r], other)

    def w_d(k):
        w = weight(k)
        for name, d in (("c0", 0), ("c1", 3), ("c2", 1), ("c3", 2)):
            arrive((name, k), w.at[region(k, slice_at(d, 1 - core))])

    def z_rows(base, d):
        return pl.ds(pl.multiple_of(base + sub * lax.rem(z + d, 8), 16), sub)

    def gather_z(tag, buf, base, c0, nc, t, dt):
        whole, first, second = pl.ds(c0, nc), pl.ds(c0, nc // 2), pl.ds(c0 + nc // 2, nc // 2)

        def step(i):
            from_left, from_right = z_rows(base, 8 - (i - 1)), z_rows(base, i - 1)
            if i > 1:
                arrive((tag, "r", i - 1), buf.at[from_left, whole])
            a = first if i == 4 else whole
            send((tag, "r", i), buf.at[from_left, a], buf.at[from_left, a], z_right)
            if i > 1:
                arrive((tag, "l", i - 1), buf.at[from_right, whole])
            b = second if i == 4 else whole
            send((tag, "l", i), buf.at[from_right, b], buf.at[from_right, b], z_left)

        def last():
            rows_at = z_rows(base, 4)
            arrive((tag, "r", 4), buf.at[rows_at, first])
            arrive((tag, "l", 4), buf.at[rows_at, second])

        for i in range(1, 5):
            at(t + (i - 1) * dt, step, i)
        at(t + 4 * dt, last)
        return t + 4 * dt

    y_rows = jnp.where(z < 4, y + 1 - 2 * lax.rem(y, 2), 3 - y)
    y_src = (dp, z, y_rows)

    def share(tag, src, buf):
        send((tag, "y"), src.at[z_rows(0, 0), :], buf.at[z_rows(rows, 0), :], y_src)

    def shared(tag, buf):
        arrive((tag, "y"), buf.at[z_rows(rows, 0), :])

    def tile(value):
        return jnp.broadcast_to(value, (8, 128))

    def top(block):
        return jnp.max(jnp.max(block, axis=0, keepdims=True), axis=1, keepdims=True)

    def peak_y(r):
        for d in range(1, 4):
            send(("py", r, d), pk_send.at[r, 0], pk_y.at[r, d - 1], y_at[d])

    def peak_z(r):
        for d in range(1, 4):
            arrive(("py", r, d), pk_y.at[r, d - 1])
        best = pk_send[r, 0]
        for d in range(3):
            best = jnp.maximum(best, pk_y[r, d])
        pk_send[r, 1] = best
        for d in range(1, 8):
            send(("pz", r, d), pk_send.at[r, 1], pk_z.at[r, d - 1], z_at[d])

    def peak_done(r):
        for d in range(1, 8):
            arrive(("pz", r, d), pk_z.at[r, d - 1])
        best = pk_send[r, 1]
        for d in range(7):
            best = jnp.maximum(best, pk_z[r, d])
        pk_send[r, 2] = best

    def pre_own():
        for load in loads[:4]:
            load.wait()

        @pl.loop(0, ff // 256)
        def _(n):
            cols = pl.ds(pl.multiple_of(n * 256, 256), 256)
            pa[:, cols] = dot_nn(tok[...], wi0[:, cols])

    def pre_chunk(k):
        cols = pl.ds(k * cw, cw)

        @pl.loop(0, ff // 256)
        def _(n):
            here = pl.ds(pl.multiple_of(n * 256, 256), 256)
            there = pl.ds(pl.multiple_of(ff + n * 256, 256), 256)
            part = dot_nn(tok[:, cols], wi1[cols, here])
            pa[:, there] = part if k == 0 else pa[:, there] + part

    def hidden_peak():
        block = 32
        best = lax.fori_loop(
            0, 2 * rows // block,
            lambda i, m: jnp.maximum(m, pa[pl.ds(pl.multiple_of(i * block, block), block), :]),
            jnp.zeros((block, 2 * ff), F32),
        )
        best = top(best)
        tokens = top(jnp.abs(tok[0:rows, :].astype(F32)))
        grads = top(jnp.abs(grd[0:rows, :].astype(F32)))
        row = lax.broadcasted_iota(jnp.int32, (8, 128), 0)
        pk_send[0, 0] = jnp.where(
            row == 0, tile(tokens), jnp.where(row == 1, tile(best * best), tile(grads))
        )
        peak_y(0)

    def scale_of(r):
        if r == 0:
            return 448.0 / (pk_send[0, 2, 1:2, 0:1] + 1e-6)
        return 57344.0 / (pk_send[1, 2, 0:1, 0:1] + 1e-6)

    def quantize(r):
        peak_done(r)
        scale = scale_of(r)
        block = 16

        @pl.loop(0, 2 * rows // block)
        def _(i):
            here = pl.ds(pl.multiple_of(i * block, block), block)
            if r == 0:
                positive = jnp.maximum(pa[here, :], 0.0)
                hq[here, :] = snap(positive * positive * scale, 3, -6, 448.0).astype(BF16)
            else:
                gq[here, :] = snap(hg[here, :] * scale, 2, -14, 57344.0).astype(BF16)

    def grad_own():
        @pl.loop(0, ff // 256)
        def _(n):
            here = pl.ds(pl.multiple_of(n * 256, 256), 256)
            hg[:, here] = dot_nt(grd[...], wo0[here, :])

    def grad_chunk(k):
        cols = pl.ds(k * cw, cw)

        @pl.loop(0, ff // 256)
        def _(n):
            here = pl.ds(pl.multiple_of(n * 256, 256), 256)
            there = pl.ds(pl.multiple_of(ff + n * 256, 256), 256)
            part = dot_nt(grd[:, cols], wo1[here, cols])
            hg[:, there] = part if k == 0 else hg[:, there] + part

    def grad_peak():
        block = 32

        def body(i, m):
            here = pl.ds(pl.multiple_of(i * block, block), block)
            pg = hg[here, :] * 2.0 * jnp.maximum(pa[here, :], 0.0)
            hg[here, :] = pg
            return jnp.maximum(m, jnp.abs(pg))

        best = lax.fori_loop(0, 2 * rows // block, body, jnp.zeros((block, 2 * ff), F32))
        pk_send[1, 0] = tile(top(best))
        peak_y(1)

    def out_chunk(o, k):
        @pl.loop(0, cw // 256)
        def _(n):
            cols = pl.ds(pl.multiple_of(k * cw + n * 256, 256), 256)
            if o == 0:
                part = dot_nn(hq[:, 0:ff], wo0[:, cols]) + dot_nn(hq[:, ff:], wo1[:, cols])
            else:
                part = dot_nt(gq[:, 0:ff], wi0[cols, :]) + dot_nt(gq[:, ff:], wi1[cols, :])
            accs[o][:, cols] = part[0:rows]
            ysend[o, :, cols] = part[rows:].astype(BF16)

        cols = pl.ds(k * cw, cw)
        a, b = pl.ds(0, half), pl.ds(half, half)
        send(("ya", o, k), ysend.at[o, a, cols], yrecv.at[o, a, cols], y_a)
        send(("yb", o, k), ysend.at[o, b, cols], yrecv.at[o, b, cols], y_b)

    def ring_step(o, k, i):
        acc = accs[o]
        c0, hw = k * cw, cw // 2
        whole, first, second = pl.ds(0, cw), pl.ds(0, hw), pl.ds(hw, hw)
        if i == 1:
            cols = pl.ds(c0, cw)
            for name, r0 in (("ya", 0), ("yb", half)):
                block = pl.ds(r0, half)
                arrive((name, o, k), yrecv.at[o, block, cols])
                acc[block, cols] = acc[block, cols] + yrecv[o, block, cols].astype(F32)
        for name, out, inn, device, d, part in (
            ("rr", send_r, recv_r, z_right, 5 - i, first),
            ("rl", send_l, recv_l, z_left, 3 + i, second),
        ):
            here = z_rows(0, d)
            if i > 1:
                span = part if i == 2 else whole
                arrive((name, o, k, i - 1), inn.at[o, k, i - 2, :, span])
            mine_ = acc[here, pl.ds(c0, cw)]
            if i == 1:
                lo = 0 if part is first else hw
                out[o, k, 0, :, lo : lo + hw] = mine_[:, lo : lo + hw].astype(BF16)
                span = part
            elif i == 2:
                for lo in (0, hw):
                    value = mine_[:, lo : lo + hw]
                    if (lo == 0) == (part is first):
                        value = value + inn[o, k, 0, :, lo : lo + hw].astype(F32)
                    out[o, k, 1, :, lo : lo + hw] = value.astype(BF16)
                span = whole
            else:
                out[o, k, i - 1] = (mine_ + inn[o, k, i - 2].astype(F32)).astype(BF16)
                span = whole
            send((name, o, k, i), out.at[o, k, i - 1, :, span], inn.at[o, k, i - 1, :, span], device)

    def finish(o, k):
        here = z_rows(0, 0)
        arrive(("rr", o, k, 4), recv_r.at[o, k, 3])
        arrive(("rl", o, k, 4), recv_l.at[o, k, 3])
        cols = pl.ds(k * cw, cw)
        total = accs[o][here, cols] + recv_r[o, k, 3].astype(F32) + recv_l[o, k, 3].astype(F32)
        obuf[o, here, cols] = (total / scale_of(o)).astype(BF16)

    def store(o):
        copy = pltpu.make_async_copy(obuf.at[o], outs[o], local_sem.at[4 + o])
        copy.start()
        loads.append(copy)

    w_y(0)
    share("tok", tok_in, tok)
    w_y(1)
    share("grd", grd_in, grd)

    for k in range(2 * CHUNKS):
        t = 4.6 + 4.3 * k
        at(t, w_a, k)
        at(t + 5.0, w_b, k)
        at(t + 10.5, w_c, k)
        at(t + 12.5, w_d, k)
        if k < CHUNKS:
            at(max(t + 12.6, 23.0 + 0.1 * k), pre_chunk, k)
        else:
            at(t + 12.6, grad_chunk, k - CHUNKS)
    at(4.5, shared, "tok", tok)
    at(6.0, shared, "grd", grd)
    t = gather_z("tok", tok, rows, 0, width, 4.55, 4.4)
    at(t + 0.1, pre_own)
    t = gather_z("grd", grd, rows, 0, width, 6.05, 6.2)
    at(t + 0.1, grad_own)
    done = 4.6 + 4.3 * 3 + 12.7
    at(done, hidden_peak)
    at(done + 3.0, peak_z, 0)
    at(done + 7.0, quantize, 0)
    first_out = done + 7.1
    grads_done = 4.6 + 4.3 * 7 + 12.7
    at(grads_done, grad_peak)
    at(grads_done + 3.0, peak_z, 1)
    at(grads_done + 7.0, quantize, 1)
    for o in range(2):
        for k in range(CHUNKS):
            if o == 0:
                t = max(first_out + 0.1 * k, 4.6 + 4.3 * (k + 4) + 12.65)
            else:
                t = grads_done + 7.1 + 1.0 * k
            at(t, out_chunk, o, k)
            t = t + 6.0
            for i in range(1, 5):
                at(t, ring_step, o, k, i)
                t += 3.0
            at(t, finish, o, k)
            t = gather_z(("out", o, k), obuf.at[o], 0, k * cw, cw, t + 0.01, 3.0)
        at(t + 0.1, store, o)

    for t, _, fn, args in sorted(events, key=lambda e: (e[0], e[1])):
        fn(*args)
        drain(40)
    row = lax.broadcasted_iota(jnp.int32, (8, 128), 0)
    peaks_out[...] = jnp.where(row < 3, pk_send[0, 2], pk_send[1, 2])
    drain(0)
    for copy in loads[4:]:
        copy.wait()


def per_device(tokens, grad_out, w_in, w_out):
    rows, width = tokens.shape
    ff = w_in.shape[1]
    hop = (2, CHUNKS, 4, rows // 8, width // CHUNKS)
    out = jax.ShapeDtypeStruct((rows, width), BF16)
    first, second, peaks = pl.pallas_call(
        kernel,
        out_shape=(out, out, jax.ShapeDtypeStruct((8, 128), F32)),
        in_specs=[pl.BlockSpec(memory_space=pl.ANY)] * 4,
        out_specs=(
            pl.BlockSpec(memory_space=pl.ANY),
            pl.BlockSpec(memory_space=pl.ANY),
            pl.BlockSpec(memory_space=pltpu.VMEM),
        ),
        scratch_shapes=[
            pltpu.VMEM((2 * rows, width), BF16),
            pltpu.VMEM((2 * rows, width), BF16),
            pltpu.VMEM((width, ff), BF16),
            pltpu.VMEM((width, ff), BF16),
            pltpu.VMEM((ff, width), BF16),
            pltpu.VMEM((ff, width), BF16),
            pltpu.VMEM((2 * rows, 2 * ff), F32),
            pltpu.VMEM((2 * rows, 2 * ff), F32),
            pltpu.VMEM((2 * rows, 2 * ff), BF16),
            pltpu.VMEM((2 * rows, 2 * ff), BF16),
            pltpu.VMEM((rows, width), F32),
            pltpu.VMEM((rows, width), F32),
            pltpu.VMEM((2, rows, width), BF16),
            pltpu.VMEM((2, rows, width), BF16),
            pltpu.VMEM(hop, BF16),
            pltpu.VMEM(hop, BF16),
            pltpu.VMEM(hop, BF16),
            pltpu.VMEM(hop, BF16),
            pltpu.VMEM((2, rows, width), BF16),
            pltpu.VMEM((2, 3, 8, 128), F32),
            pltpu.VMEM((2, 3, 8, 128), F32),
            pltpu.VMEM((2, 7, 8, 128), F32),
            pltpu.SemaphoreType.DMA((6,)),
            pltpu.SemaphoreType.DMA((DMAS,)),
            pltpu.SemaphoreType.DMA((DMAS,)),
        ],
        compiler_params=pltpu.CompilerParams(
            collective_id=0, has_side_effects=True, vmem_limit_bytes=58 * 2**20
        ),
    )(tokens, grad_out, w_in, w_out)
    return first, second, jnp.log(peaks[:4, 0] + 1e-6)


def solution(mesh):
    return jax.shard_map(
        per_device,
        mesh=mesh,
        in_specs=(
            P(("dp", "tensor"), None),
            P(("dp", "tensor"), None),
            P(None, ("pipe", "tensor")),
            P(("pipe", "tensor"), None),
        ),
        out_specs=(P(("dp", "tensor"), None), P(("dp", "tensor"), None), P("dp")),
        check_vma=False,
    )
```
